256 devices in a mesh: ctx: 32 (over x_hi, z, core), grp: 4 (over y), dp: 2 (over x_lo).
Axes of the slice: x: 4 (x_hi: 2, x_lo: 2; x = x_hi * 2 + x_lo), y: 4, z: 8, core: 2. Of those that a mesh axis runs over, the one named last changes fastest.
Arguments:
- query_rows: bfloat16 [2, 4096, 4096], P('dp', 'ctx', 'grp'), may hold values from -64 to 64, as said below
- key_rows: bfloat16 [2, 4096, 4096], P('dp', 'ctx', 'grp'), may hold values from -8 to 8, as said below
- value_rows: bfloat16 [2, 4096, 4096], P('dp', 'ctx', 'grp'), may hold values from -6 to 6
- seq_length: int32 [2], P('dp'), may hold values from 1024 to 4096
- out_weight: bfloat16 [4096, 2048], P('grp'), may hold values from -0.09375 to 0.09375
- out_grad: bfloat16 [2, 4096, 2048], P('dp', ('ctx', 'grp')), may hold values from -0.75 to 0.75
Outputs:
- block_out: bfloat16 [2, 4096, 2048], P('dp', ('ctx', 'grp'))
- weight_grad: float32 [4096, 2048], P('grp', ('ctx', 'dp'))
The draws below stay inside these ranges and needn't reach their ends.
Inputs may be any that keep to these rules, and one draw needn't show every extreme that they name: `query_rows`: every entry lies between the bounds given. `key_rows`: every entry lies between the bounds given.
All inputs are finite; a program needn't handle non-finite values.
Results may differ from the reference program's by a relative error of at most 0.015.
Values may be sent and summed in bfloat16 or wider, within the bound.
No kernel may reach another device: no remote copies, remote signals or barrier semaphores. Data moves between devices by JAX's collectives and lax.ppermute only.
A program may use at most 64 MiB of HBM per device.

```python
import math
import jax
import jax.numpy as jnp
from jax import lax

HEADS = 16
HEAD_DIM = 256
D_OUT = 2048
SEQS = 2
SEQ_LEN = 4096


def shared_keys(key):
    rows = jax.random.normal(key, (SEQS, SEQ_LEN, HEADS * HEAD_DIM), jnp.float32)
    return 2.0 * jnp.clip(rows, -4.0, 4.0)


def draw_key_rows(key, part):
    rows = shared_keys(key)
    return rows.astype(jnp.bfloat16)


def draw_query_rows(key, part):
    key = jax.random.fold_in(key, 3)
    shape = (SEQS, SEQ_LEN, HEADS * HEAD_DIM)
    rows = 1.5 * jnp.clip(jax.random.normal(key, shape, jnp.float32), -4.0, 4.0)
    return rows.astype(jnp.bfloat16)


def with_spikes(result, key, source, target, blocks, factor):
    owner, partner = [(jnp.arange(result.shape[dim]) // (result.shape[dim] // blocks)).reshape([-1 if axis == dim else 1 for axis in range(result.ndim)]) for dim in (source, target)]
    chosen = jax.random.permutation(key, blocks)[partner]
    strong = (owner == chosen) | (owner == (partner + blocks // 2) % blocks)
    return jnp.where(strong, factor * result, result)


def shard_levels(rng, extent, shards, least, high):
    def one(dim, blocks):
        draws = jax.random.uniform(jax.random.fold_in(jax.random.fold_in(rng, 6), dim), (blocks,), jnp.float32, least / len(shards), high / len(shards))
        return jnp.repeat(jnp.exp(draws), extent[dim] // blocks).reshape((-1,) + (1,) * (len(extent) - dim - 1))

    loudness = one(*shards[0])
    for cut in shards[1:]:
        loudness = loudness * one(*cut)
    return loudness


def centred(stream_key, extent, deviation, limit, split=(), kind=jnp.bfloat16):
    drawn = deviation * jax.random.normal(stream_key, extent, jnp.float32)
    if split:
        drawn = drawn * shard_levels(stream_key, extent, split, -0.22, 0.18)
    return jnp.clip(drawn, -limit, limit).astype(kind)


def heavy_noise(key, dims, scale, limit, cuts, heavy, dtype=jnp.bfloat16):
    values = scale * jax.random.normal(key, dims, jnp.float32)
    if cuts:
        values = values * shard_levels(key, dims, cuts, -0.22, 0.18)
    return jnp.clip(with_spikes(values, jax.random.fold_in(key, 3), *heavy), -limit, limit).astype(dtype)


def setup_inputs(seed: int = 0) -> dict:
    seeds = jax.random.split(jax.random.key(seed), 7)
    query_rows = draw_query_rows(jax.random.fold_in(seeds[6], 71), 0)
    key_rows = draw_key_rows(jax.random.fold_in(seeds[6], 71), 0)
    value_rows = centred(seeds[2], (SEQS, SEQ_LEN, HEADS * HEAD_DIM), 1.0, 6.0, ((0, 2), (1, 32), (2, 4)))
    seq_length = jax.random.randint(seeds[3], (SEQS,), SEQ_LEN // 4, SEQ_LEN + 1).astype(jnp.int32)
    out_weight = centred(seeds[4], (HEADS * HEAD_DIM, D_OUT), (HEADS * HEAD_DIM) ** -0.5, 0.09375, ((0, 4),))
    out_grad = heavy_noise(seeds[5], (SEQS, SEQ_LEN, D_OUT), (3.0 / (SEQS * SEQ_LEN) ** 0.5), 0.75, ((0, 2), (1, 128)), (1, 2, 128, 5.5))
    return dict(query_rows=query_rows, key_rows=key_rows, value_rows=value_rows, seq_length=seq_length, out_weight=out_weight, out_grad=out_grad)


masked_score = -1e+30

def reference(query_rows, key_rows, value_rows, seq_length, out_weight, out_grad):
    scale = 1.0 / math.sqrt(HEAD_DIM)
    positions = jnp.arange(SEQ_LEN)
    outputs = []
    grad_total = jnp.zeros((HEADS * HEAD_DIM, D_OUT), jnp.float32)
    for seq_index in range(SEQS):
        live_keys = positions < seq_length[seq_index]

        def one_head(operands):
            query_head, key_head, value_head = operands
            scores = jnp.dot(query_head, key_head.T, preferred_element_type=jnp.float32) * scale
            scores = jnp.where(live_keys[None, :], scores, masked_score)
            row_best = lax.optimization_barrier(jnp.max(scores, axis=1, keepdims=True))
            exp_terms = jnp.where(live_keys[None, :], jnp.exp(scores - row_best), 0.0)
            row_total = lax.optimization_barrier(jnp.sum(exp_terms, axis=1, keepdims=True))
            weights = exp_terms.astype(jnp.bfloat16)
            numerator = jnp.dot(weights, value_head, preferred_element_type=jnp.float32)
            return numerator / row_total

        def by_heads(array):
            return array[seq_index].reshape(SEQ_LEN, HEADS, HEAD_DIM).transpose(1, 0, 2)
        heads_out = lax.map(one_head, (by_heads(query_rows), by_heads(key_rows), by_heads(value_rows)))
        context = heads_out.transpose(1, 0, 2).reshape(SEQ_LEN, HEADS * HEAD_DIM)
        context = jnp.where(live_keys[:, None], context, 0.0).astype(jnp.bfloat16)
        outputs.append(jnp.dot(context, out_weight, preferred_element_type=jnp.float32).astype(jnp.bfloat16))
        grad_total = grad_total + jnp.dot(context.T, out_grad[seq_index], preferred_element_type=jnp.float32)
    return (jnp.stack(outputs), grad_total)
```

```python
import math

import jax
import jax.numpy as jnp
from jax import lax
from jax.experimental import pallas as pl
from jax.experimental.pallas import tpu as pltpu
from jax.sharding import Mesh, PartitionSpec as P

HEAD_DIM = 256
SPLIT = (("xh", 2), ("zq", 4), ("zr", 2), ("core", 2), ("y", 4), ("xl", 2))
AXES = tuple(name for name, _ in SPLIT)
SIZE = dict(SPLIT)
MASKED = -1e30
BF = jnp.bfloat16
F32 = jnp.float32


def moved(value, shift):
    names = tuple(shift)
    sizes = [SIZE[n] for n in names]
    count = math.prod(sizes)
    pairs = []
    for source in range(count):
        rest, place = source, []
        for s in reversed(sizes):
            place.append(rest % s)
            rest //= s
        place = place[::-1]
        target = 0
        for p, s, n in zip(place, sizes, names):
            target = target * s + (p + shift[n]) % s
        pairs.append((source, target))
    return lax.ppermute(value, names, pairs)


def scores_body(q0, q1, k0, k1, k2, k3, bias, p_out, stat_out):
    tile = p_out.shape[0]
    own = pl.program_id(0) < pl.num_programs(0) // 2

    def run(q_ref):
        q = q_ref[...]
        parts = []
        for i, k in enumerate((k0, k1, k2, k3)):
            s = lax.dot_general(q, k[...], (((1,), (1,)), ((), ())), preferred_element_type=F32)
            width = k.shape[0]
            parts.append(s * (math.log2(math.e) / math.sqrt(HEAD_DIM)) + bias[:, i * width : (i + 1) * width])
        top = parts[0].max(axis=1, keepdims=True)
        for s in parts[1:]:
            top = jnp.maximum(top, s.max(axis=1, keepdims=True))
        total = jnp.zeros((tile, 1), F32)
        for i, s in enumerate(parts):
            e = jnp.exp2(s - top)
            total += e.sum(axis=1, keepdims=True)
            width = s.shape[1]
            p_out[:, i * width : (i + 1) * width] = e.astype(BF)
        stat_out[:, :128] = jnp.broadcast_to(top, (tile, 128))
        stat_out[:, 128:] = jnp.broadcast_to(total, (tile, 128))

    @pl.when(own)
    def _():
        run(q0)

    @pl.when(jnp.logical_not(own))
    def _():
        run(q1)


def score_kernel(q_own, q_other, ks, bias):
    half = q_own.shape[0]
    tile = 256
    steps = half // tile
    keys = sum(k.shape[0] for k in ks)
    return pl.pallas_call(
        scores_body,
        grid=(2 * steps,),
        in_specs=[
            pl.BlockSpec((tile, HEAD_DIM), lambda i: (jnp.minimum(i, steps - 1), 0)),
            pl.BlockSpec((tile, HEAD_DIM), lambda i: (jnp.maximum(i - steps, 0), 0)),
        ]
        + [pl.BlockSpec(k.shape, lambda i: (0, 0)) for k in ks]
        + [pl.BlockSpec((1, keys), lambda i: (0, 0))],
        out_specs=[
            pl.BlockSpec((tile, keys), lambda i: (i, 0)),
            pl.BlockSpec((tile, 256), lambda i: (i, 0)),
        ],
        out_shape=[
            jax.ShapeDtypeStruct((2 * half, keys), BF),
            jax.ShapeDtypeStruct((2 * half, 256), F32),
        ],
        compiler_params=pltpu.CompilerParams(vmem_limit_bytes=40 * 2**20),
        cost_estimate=pl.CostEstimate(
            flops=2 * 2 * half * keys * HEAD_DIM, bytes_accessed=2 * 2 * half * keys, transcendentals=2 * half * keys
        ),
    )(q_own, q_other, *ks, bias)


def values_body(p_ref, v0, v1, v2, v3, mine, theirs, live, out):
    acc = jnp.zeros(out.shape, F32)
    for i, v in enumerate((v0, v1, v2, v3)):
        width = v.shape[0]
        acc += jnp.dot(p_ref[:, i * width : (i + 1) * width], v[...], preferred_element_type=F32)
    top_mine, top_theirs = mine[:, :128], theirs[:, :128]
    top = jnp.maximum(top_mine, top_theirs)
    fade = jnp.exp2(top_mine - top)
    total = mine[:, 128:] * fade + theirs[:, 128:] * jnp.exp2(top_theirs - top)
    factor = fade / total * live[...]
    out[:, :128] = acc[:, :128] * factor
    out[:, 128:] = acc[:, 128:] * factor


def value_kernel(p, vs, mine, theirs, live):
    rows, keys = p.shape
    tile = 256
    return pl.pallas_call(
        values_body,
        grid=(rows // tile,),
        in_specs=[pl.BlockSpec((tile, keys), lambda i: (i, 0))]
        + [pl.BlockSpec(v.shape, lambda i: (0, 0)) for v in vs]
        + [pl.BlockSpec((tile, 256), lambda i: (i, 0))] * 2
        + [pl.BlockSpec((tile, 1), lambda i: (i, 0))],
        out_specs=pl.BlockSpec((tile, HEAD_DIM), lambda i: (i, 0)),
        out_shape=jax.ShapeDtypeStruct((rows, HEAD_DIM), F32),
        compiler_params=pltpu.CompilerParams(vmem_limit_bytes=40 * 2**20),
        cost_estimate=pl.CostEstimate(flops=2 * rows * keys * HEAD_DIM, bytes_accessed=4 * rows * keys, transcendentals=0),
    )(p, *vs, mine, theirs, live)


def local(query_rows, key_rows, value_rows, seq_length, out_weight, out_grad):
    query, key, value = query_rows[0], key_rows[0], value_rows[0]
    length = seq_length[0]
    count = query.shape[0]
    xh, zq, zr, core, y = (lax.axis_index(n) for n in ("xh", "zq", "zr", "core", "y"))

    def head_of(array, steps):
        return lax.dynamic_slice_in_dim(array, ((zq + steps) % 4) * HEAD_DIM, HEAD_DIM, 1)

    kq = [jnp.stack([head_of(key, d), head_of(query, d)]) for d in range(4)]
    kq = [kq[0]] + [moved(kq[d], {"zq": d}) for d in (1, 2, 3)]
    vv = [head_of(value, 0)] + [moved(head_of(value, d), {"zq": d}) for d in (1, 2, 3)]
    q_own = jnp.concatenate([pair[1] for pair in kq])
    k_own = jnp.concatenate([pair[0] for pair in kq])
    v_own = jnp.concatenate(vv)
    q_other = moved(q_own, {"core": 1})
    quad = ({"zr": 1}, {"xh": 1}, {"xh": 1, "zr": 1})
    ks = [k_own] + [moved(k_own, s) for s in quad]
    vs = [v_own] + [moved(v_own, s) for s in quad]

    def positions(xh, zr, core):
        source = (zq - jnp.arange(4)) % 4
        block = xh * 16 + source * 4 + zr * 2 + core
        return (block[:, None] * count + jnp.arange(count)[None, :]).reshape(-1)

    key_place = jnp.concatenate(
        [positions(xh, zr, core), positions(xh, 1 - zr, core), positions(1 - xh, zr, core), positions(1 - xh, 1 - zr, core)]
    )
    bias = jnp.where(key_place < length, 0.0, MASKED).astype(F32)[None, :]
    query_place = jnp.concatenate([positions(xh, zr, core), positions(xh, zr, 1 - core)])
    live = (query_place < length).astype(F32)[:, None]

    weights, mine = score_kernel(q_own, q_other, ks, bias)
    theirs_swapped = moved(mine, {"core": 1})
    half = q_own.shape[0]
    theirs = jnp.concatenate([theirs_swapped[half:], theirs_swapped[:half]])
    partial = value_kernel(weights, vs, mine, theirs, live)
    from_other = moved(partial, {"core": 1})
    context_own = (partial[:half] + from_other[half:]).astype(BF)
    context_other = (partial[half:] + from_other[:half]).astype(BF)

    grad = out_grad[0]
    rows, width = grad.shape
    grad = grad.reshape(rows, 16, 2, 64)
    keep = lax.dynamic_index_in_dim(grad, core, 2, keepdims=False).reshape(rows, width // 2)
    give = lax.dynamic_index_in_dim(grad, 1 - core, 2, keepdims=False).reshape(rows, width // 2)
    grad = jnp.stack([keep, moved(give, {"core": 1})])
    grad = jnp.stack([grad] + [moved(grad, {"zq": d}) for d in (1, 2, 3)])
    grads = [grad] + [moved(grad, {"y": d}) for d in (1, 2, 3)]
    contexts = jnp.stack([context_own, context_other]).reshape(2, 4, 4, rows, HEAD_DIM)
    total = jnp.zeros((width // 2, HEAD_DIM), F32)
    for d in range(4):
        part = lax.dynamic_index_in_dim(contexts, (y - d) % 4, 2, keepdims=False)
        part = part.transpose(1, 0, 2, 3).reshape(8 * rows, HEAD_DIM)
        total += lax.dot_general(
            grads[d].reshape(8 * rows, width // 2), part, (((0,), (0,)), ((), ())), preferred_element_type=F32
        )
    xl = lax.axis_index("xl")
    total = total.reshape(2, 4, 2, 2, 32, HEAD_DIM)

    def for_x(dh, dl):
        part = lax.dynamic_index_in_dim(total, (xh + dh) % 2, 0, keepdims=False)
        return lax.dynamic_index_in_dim(part, (xl + dl) % 2, 2, keepdims=False)

    summed = for_x(0, 0)
    for dh, dl in ((0, 1), (1, 0), (1, 1)):
        summed += moved(for_x(dh, dl).astype(BF), {"xh": dh, "xl": dl}).astype(F32)
    keep = lax.dynamic_index_in_dim(summed, zr, 1, keepdims=False)
    give = lax.dynamic_index_in_dim(summed, 1 - zr, 1, keepdims=False)
    summed = keep + moved(give.astype(BF), {"zr": 1}).astype(F32)

    def for_zq(steps):
        return lax.dynamic_index_in_dim(summed, (zq + steps) % 4, 0, keepdims=False)

    heads = [for_zq(0)] + [moved(for_zq(d), {"zq": d}) for d in (1, 2, 3)]
    weight_grad = jnp.zeros((4, 32, HEAD_DIM), F32)
    for d, part in enumerate(heads):
        weight_grad = lax.dynamic_update_index_in_dim(weight_grad, part, (zq - d) % 4, 0)
    weight_grad = weight_grad.transpose(0, 2, 1).reshape(4 * HEAD_DIM, 32)

    back = context_own.reshape(4, count, HEAD_DIM)
    mine_back = jnp.zeros((count, 4 * HEAD_DIM), BF)
    for d in range(4):
        part = back[d] if d == 0 else moved(back[d], {"zq": -d})
        mine_back = lax.dynamic_update_slice_in_dim(mine_back, part, ((zq + d) % 4) * HEAD_DIM, 1)
    projected = jnp.dot(mine_back, out_weight, preferred_element_type=F32).reshape(4, rows, width)

    def for_y(steps):
        return lax.dynamic_index_in_dim(projected, (y + steps) % 4, 0, keepdims=False)

    block = for_y(0)
    for d in (1, 2, 3):
        block += moved(for_y(d).astype(BF), {"y": d}).astype(F32)
    return block.astype(BF)[None], weight_grad


def solution(mesh):
    fine = Mesh(mesh.devices.reshape([s for _, s in SPLIT]), AXES)
    ctx = ("xh", "zq", "zr", "core")
    in_specs = (
        P("xl", ctx, "y"),
        P("xl", ctx, "y"),
        P("xl", ctx, "y"),
        P("xl"),
        P("y", None),
        P("xl", ctx + ("y",), None),
    )
    out_specs = (P("xl", ctx + ("y",), None), P("y", ctx + ("xl",)))
    return jax.shard_map(local, mesh=fine, in_specs=in_specs, out_specs=out_specs, check_vma=False)
```

```python
import math

import jax
import jax.numpy as jnp
from jax import lax
from jax.experimental import pallas as pl
from jax.experimental.pallas import tpu as pltpu
from jax.sharding import Mesh, PartitionSpec as P

HEAD_DIM = 256
SPLIT = (("xh", 2), ("zq", 4), ("zr", 2), ("core", 2), ("y", 4), ("xl", 2))
AXES = tuple(name for name, _ in SPLIT)
SIZE = dict(SPLIT)
MASKED = -1e30
BF = jnp.bfloat16
F32 = jnp.float32
VMEM = 14 * 2**20


def moved(value, **shift):
    names = tuple(shift)
    sizes = [SIZE[n] for n in names]
    count = math.prod(sizes)
    pairs = []
    for source in range(count):
        rest, place = source, []
        for s in reversed(sizes):
            place.append(rest % s)
            rest //= s
        place = place[::-1]
        target = 0
        for p, s, n in zip(place, sizes, names):
            target = target * s + (p + shift[n]) % s
        pairs.append((source, target))
    return lax.ppermute(value, names, pairs)


def after(value, *earlier):
    return lax.optimization_barrier((value, *earlier))[0]


def attend_body(q_ref, k0, k1, k2, k3, v0, v1, v2, v3, bias, out, *stat_out):
    tile = q_ref.shape[0]
    q = q_ref[...]
    parts = []
    for i, k in enumerate((k0, k1, k2, k3)):
        s = lax.dot_general(q, k[...], (((1,), (1,)), ((), ())), preferred_element_type=F32)
        width = k.shape[0]
        parts.append(s * (math.log2(math.e) / math.sqrt(HEAD_DIM)) + bias[:, i * width : (i + 1) * width])
    top = parts[0].max(axis=1, keepdims=True)
    for s in parts[1:]:
        top = jnp.maximum(top, s.max(axis=1, keepdims=True))
    total = jnp.zeros((tile, 1), F32)
    acc = jnp.zeros((tile, HEAD_DIM), F32)
    for s, v in zip(parts, (v0, v1, v2, v3)):
        e = jnp.exp2(s - top)
        total += e.sum(axis=1, keepdims=True)
        acc += jnp.dot(e.astype(BF), v[...], preferred_element_type=F32)
    if stat_out:
        out[...] = acc / total
        stat_out[0][:4, :] = jnp.broadcast_to(top, (tile, 128)).T[:4]
        stat_out[0][4:, :] = jnp.broadcast_to(total, (tile, 128)).T[:4]
        return
    step = pl.program_id(0)
    out[pl.ds(pl.multiple_of(step * tile, tile), tile), :] = (acc / total).astype(BF)
    lines = []
    for stat in (top, total):
        left = jnp.broadcast_to(stat, (tile, 128)).T[:1]
        for _ in range(3):
            lines.append(left.astype(BF).astype(F32))
            left = left - lines[-1]
        lines.append(jnp.zeros((5, tile), F32))
    below = pl.multiple_of(pl.num_programs(0) * tile + step * 16, 16)
    out[pl.ds(below, 16), :] = jnp.concatenate(lines).astype(BF)


def attend(q, pieces, bias, dtype):
    rows = q.shape[0]
    tile = 256
    steps = rows // tile
    part = pieces[0].shape[0] // 4
    keys = 4 * part
    if dtype == F32:
        out_specs = [pl.BlockSpec((tile, HEAD_DIM), lambda i: (i, 0)), pl.BlockSpec((8, tile), lambda i: (0, i))]
        out_shape = [jax.ShapeDtypeStruct((rows, HEAD_DIM), F32), jax.ShapeDtypeStruct((8, rows), F32)]
    else:
        out_shape = jax.ShapeDtypeStruct((rows + 16 * steps, HEAD_DIM), BF)
        out_specs = pl.BlockSpec(out_shape.shape, lambda i: (0, 0))
    return pl.pallas_call(
        attend_body,
        grid=(steps,),
        in_specs=[pl.BlockSpec((tile, HEAD_DIM), lambda i: (i, 0))]
        + [pl.BlockSpec((part, HEAD_DIM), lambda i, at=at: (at, 0)) for at in (0, 0, 2, 2, 1, 1, 3, 3)]
        + [pl.BlockSpec((1, keys), lambda i: (0, 0))],
        out_specs=out_specs,
        out_shape=out_shape,
        compiler_params=pltpu.CompilerParams(vmem_limit_bytes=VMEM),
        cost_estimate=pl.CostEstimate(
            flops=4 * rows * keys * HEAD_DIM, bytes_accessed=4 * keys * HEAD_DIM, transcendentals=rows * keys
        ),
    )(q, *pieces * 4, bias)


def combine_body(mine, mine_stat, theirs, theirs_stat, live, out):
    def joined(at):
        parts = theirs_stat[at : at + 8, :].astype(F32)
        return parts[0:1] + parts[1:2] + parts[2:3]

    top_mine, top_theirs = mine_stat[0:1], joined(0)
    top = jnp.maximum(top_mine, top_theirs)
    part_mine = mine_stat[4:5] * jnp.exp2(top_mine - top)
    part_theirs = joined(8) * jnp.exp2(top_theirs - top)
    factor = live[...] / (part_mine + part_theirs)
    tile = out.shape[0]

    def down(row):
        wide = jnp.broadcast_to(row, (128, tile)).T
        return jnp.concatenate([wide, wide], axis=1)

    out[...] = (mine[...] * down(part_mine * factor) + theirs[...].astype(F32) * down(part_theirs * factor)).astype(BF)


def combine(mine, mine_stat, theirs, live):
    rows = mine.shape[0]
    tile = 256
    return pl.pallas_call(
        combine_body,
        grid=(rows // tile,),
        in_specs=[
            pl.BlockSpec((tile, HEAD_DIM), lambda i: (i, 0)),
            pl.BlockSpec((8, tile), lambda i: (0, i)),
            pl.BlockSpec((tile, HEAD_DIM), lambda i: (i, 0)),
            pl.BlockSpec((16, tile), lambda i: (rows // 16 + i, 0)),
            pl.BlockSpec((1, tile), lambda i: (0, i)),
        ],
        out_specs=pl.BlockSpec((tile, HEAD_DIM), lambda i: (i, 0)),
        out_shape=jax.ShapeDtypeStruct((rows, HEAD_DIM), BF),
        compiler_params=pltpu.CompilerParams(vmem_limit_bytes=VMEM // 2),
    )(mine, mine_stat, theirs, theirs, live)


def columns_body(grad, swap, out):
    for xh in range(2):
        for zq in range(4):
            at = (xh * 4 + zq) * 256
            both = jnp.dot(grad[:, at : at + 256], swap[...], preferred_element_type=F32).astype(BF)
            for xl in range(2):
                out[xh, xl, :, zq * 128 : (zq + 1) * 128] = both[:, xl * 128 : (xl + 1) * 128]


def by_owner(grad):
    rows, width = grad.shape
    place = jnp.arange(256)
    source = place % 128 // 32 * 64 + place // 128 * 32 + place % 32
    swap = (place[:, None] == source[None, :]).astype(BF)
    return pl.pallas_call(
        columns_body,
        out_shape=jax.ShapeDtypeStruct((2, 2, rows, width // 4), BF),
        compiler_params=pltpu.CompilerParams(vmem_limit_bytes=VMEM // 2),
        cost_estimate=pl.CostEstimate(flops=2 * rows * width * 256, bytes_accessed=2**19, transcendentals=0),
    )(grad, swap)


def beside(value, dh, dl):
    return moved(value, xh=dh, xl=dl) if dh or dl else value


def local(query_rows, key_rows, value_rows, seq_length, out_weight, out_grad):
    query, key, value = query_rows[0], key_rows[0], value_rows[0]
    length = seq_length[0]
    count = query.shape[0]
    xh, zq, zr, core, y, xl = (lax.axis_index(n) for n in AXES)

    def head_of(array, steps):
        return lax.dynamic_slice_in_dim(array, ((zq + steps) % 4) * HEAD_DIM, HEAD_DIM, 1)

    sent = {d: jnp.concatenate([head_of(key, d), head_of(query, d), head_of(value, d)]) for d in range(4)}
    sent = {d: moved(sent[d], zq=d) if d else sent[d] for d in (1, 3, 2, 0)}
    k_own, q_own, v_own = (
        jnp.concatenate([sent[d][i * count : (i + 1) * count] for d in range(4)]) for i in range(3)
    )
    rows, width = out_grad.shape[1:]
    grad = by_owner(out_grad[0])

    sides = ((0, 0), (0, 1), (1, 1), (1, 0))

    def for_x(dh, dl):
        part = lax.dynamic_index_in_dim(grad, (xh + dh) % 2, 0, keepdims=False)
        return lax.dynamic_index_in_dim(part, (xl + dl) % 2, 0, keepdims=False)

    grad = jnp.stack([beside(for_x(*side), *side) for side in sides])

    def positions(xh, zr, core):
        source = (zq - jnp.arange(4)) % 4
        block = xh * 16 + source * 4 + zr * 2 + core
        return (block[:, None] * count + jnp.arange(count)[None, :]).reshape(-1)

    key_place = jnp.concatenate(
        [positions(xh, zr, core), positions(xh, zr, 1 - core), positions(1 - xh, zr, core), positions(1 - xh, zr, 1 - core)]
    )
    bias = jnp.where(key_place < length, 0.0, MASKED).astype(F32)[None, :]
    live = (positions(xh, zr, core) < length).astype(F32)[None, :]
    grad_y = {0: grad, 1: moved(grad, y=1), 3: moved(grad, y=3)}
    k_own, q_own, v_own, bias, live, grad_y = lax.optimization_barrier((k_own, q_own, v_own, bias, live, grad_y))

    own = jnp.concatenate([k_own, v_own])
    other = moved(own, xh=1)
    q_other = moved(q_own, zr=1)
    other, q_other = lax.optimization_barrier((other, q_other))
    pieces = jnp.concatenate([own, other])
    pieces = (pieces, moved(pieces, core=1))

    theirs = attend(q_other, pieces, bias, BF)
    theirs = moved(theirs, zr=1)
    mine, mine_stat = attend(q_own, pieces, bias, F32)
    grad_y[2] = moved(after(grad_y[0], mine_stat), y=2)
    context = combine(mine, mine_stat, theirs, live)

    back = context.reshape(4, count, HEAD_DIM)
    mine_back = jnp.zeros((count, 4 * HEAD_DIM), BF)
    for d in (0, 1, 3, 2):
        part = moved(back[d], zq=-d) if d else back[d]
        mine_back = lax.dynamic_update_slice_in_dim(mine_back, part, ((zq + d) % 4) * HEAD_DIM, 1)

    grad_y[2] = after(grad_y[2], context)
    grad_rows = jnp.zeros((4, 4, rows, width // 4), BF)
    for d in range(4):
        grad_rows = lax.dynamic_update_index_in_dim(grad_rows, grad_y[d], (y - d) % 4, 1)
    grad_rows = grad_rows.reshape(16 * rows, width // 4)

    gathered = jnp.concatenate([beside(mine_back, *side) for side in sides])
    projected = jnp.dot(mine_back, out_weight, preferred_element_type=F32).astype(BF).reshape(4, rows, width)
    gathered, projected = lax.optimization_barrier((gathered, projected))
    total = lax.dot_general(grad_rows, gathered, (((0,), (0,)), ((), ())), preferred_element_type=F32)
    total = total.reshape(4, 2, 2, 32, 4 * HEAD_DIM)
    for axis, name, place in ((2, "core", core), (1, "zr", zr)):
        keep = lax.dynamic_index_in_dim(total, place, axis, keepdims=False)
        give = lax.dynamic_index_in_dim(total, 1 - place, axis, keepdims=False)
        total = keep + moved(give.astype(BF), **{name: 1}).astype(F32)
    weight_grad = lax.dynamic_index_in_dim(total, zq, 0, keepdims=False)
    for d in (1, 3, 2):
        part = lax.dynamic_index_in_dim(total, (zq + d) % 4, 0, keepdims=False)
        weight_grad += moved(part.astype(BF), zq=d).astype(F32)


    def for_y(steps):
        return lax.dynamic_index_in_dim(projected, (y + steps) % 4, 0, keepdims=False)

    block = for_y(0).astype(F32)
    for d in (1, 3, 2):
        block += moved(for_y(d), y=d).astype(F32)
    return block.astype(BF)[None], weight_grad.T


def solution(mesh):
    fine = Mesh(mesh.devices.reshape([s for _, s in SPLIT]), AXES)
    ctx = ("xh", "zq", "zr", "core")
    in_specs = (
        P("xl", ctx, "y"),
        P("xl", ctx, "y"),
        P("xl", ctx, "y"),
        P("xl"),
        P("y", None),
        P("xl", ctx + ("y",), None),
    )
    out_specs = (P("xl", ctx + ("y",), None), P("y", ctx + ("xl",)))
    return jax.shard_map(local, mesh=fine, in_specs=in_specs, out_specs=out_specs, check_vma=False)
```

```python
import functools
import math

import jax
import jax.numpy as jnp
from jax import lax
from jax.experimental import pallas as pl
from jax.experimental.pallas import tpu as pltpu
from jax.sharding import Mesh, PartitionSpec as P

HEAD_DIM = 256
SPLIT = (("xh", 2), ("zq", 4), ("zr", 2), ("core", 2), ("y", 4), ("xl", 2))
AXES = tuple(name for name, _ in SPLIT)
SIZE = dict(SPLIT)
MASKED = -1e30
BF = jnp.bfloat16
F32 = jnp.float32
VMEM = 14 * 2**20


def moved(value, **shift):
    names = tuple(shift)
    sizes = [SIZE[n] for n in names]
    count = math.prod(sizes)
    pairs = []
    for source in range(count):
        rest, place = source, []
        for s in reversed(sizes):
            place.append(rest % s)
            rest //= s
        place = place[::-1]
        target = 0
        for p, s, n in zip(place, sizes, names):
            target = target * s + (p + shift[n]) % s
        pairs.append((source, target))
    return lax.ppermute(value, names, pairs)


def after(value, *earlier):
    return lax.optimization_barrier((value, *earlier))[0]


def attend_body(q_ref, k0, k1, v0, v1, bias, *refs, first, packed):
    tile = q_ref.shape[0]
    q = q_ref[...]
    if first:
        out, stat_out = refs
        acc = jnp.zeros((tile, HEAD_DIM), F32)
        total = jnp.zeros((tile, 1), F32)
        top = jnp.full((tile, 1), -jnp.inf, F32)
    else:
        acc_in, stat_in, out, *stat_out = refs

        def down(row):
            return jnp.broadcast_to(row, (128, tile)).T[:, :1]

        top, total = down(stat_in[0:1]), down(stat_in[4:5])
    parts = []
    new_top = top
    for i, k in enumerate((k0, k1)):
        s = lax.dot_general(q, k[...], (((1,), (1,)), ((), ())), preferred_element_type=F32)
        width = k.shape[0]
        parts.append(s * (math.log2(math.e) / math.sqrt(HEAD_DIM)) + bias[:, i * width : (i + 1) * width])
        new_top = jnp.maximum(new_top, parts[-1].max(axis=1, keepdims=True))
    if not first:
        fade = jnp.exp2(top - new_top)
        total = total * fade
        acc = acc_in[...] * fade
    top = new_top
    for s, v in zip(parts, (v0, v1)):
        e = jnp.exp2(s - top)
        total += e.sum(axis=1, keepdims=True)
        acc += jnp.dot(e.astype(BF), v[...], preferred_element_type=F32)
    if not packed:
        out[...] = acc if first else acc / total
        stat_out = stat_out if first else stat_out[0]
        stat_out[:4, :] = jnp.broadcast_to(top, (tile, 128)).T[:4]
        stat_out[4:, :] = jnp.broadcast_to(total, (tile, 128)).T[:4]
        return
    step = pl.program_id(0)
    out[pl.ds(pl.multiple_of(step * tile, tile), tile), :] = (acc / total).astype(BF)
    lines = []
    for stat in (top, total):
        left = jnp.broadcast_to(stat, (tile, 128)).T[:1]
        for _ in range(3):
            lines.append(left.astype(BF).astype(F32))
            left = left - lines[-1]
        lines.append(jnp.zeros((5, tile), F32))
    below = pl.multiple_of(pl.num_programs(0) * tile + step * 16, 16)
    out[pl.ds(below, 16), :] = jnp.concatenate(lines).astype(BF)


def attend(q, pieces, bias, before=None, packed=False):
    rows = q.shape[0]
    tile = 256
    steps = rows // tile
    part = pieces[0].shape[0] // 2
    first = before is None
    rows_spec = pl.BlockSpec((tile, HEAD_DIM), lambda i: (i, 0))
    stat_spec = pl.BlockSpec((8, tile), lambda i: (0, i))
    if packed:
        out_shape = jax.ShapeDtypeStruct((rows + 16 * steps, HEAD_DIM), BF)
        out_specs = pl.BlockSpec(out_shape.shape, lambda i: (0, 0))
    else:
        out_specs = [rows_spec, stat_spec]
        out_shape = [jax.ShapeDtypeStruct((rows, HEAD_DIM), F32), jax.ShapeDtypeStruct((8, rows), F32)]
    return pl.pallas_call(
        functools.partial(attend_body, first=first, packed=packed),
        grid=(steps,),
        in_specs=[rows_spec]
        + [pl.BlockSpec((part, HEAD_DIM), lambda i, at=at: (at, 0)) for at in (0, 0, 1, 1)]
        + [pl.BlockSpec((1, 2 * part), lambda i: (0, 0 if first else 1))]
        + ([] if first else [rows_spec, stat_spec]),
        out_specs=out_specs,
        out_shape=out_shape,
        compiler_params=pltpu.CompilerParams(vmem_limit_bytes=VMEM),
        cost_estimate=pl.CostEstimate(
            flops=8 * rows * part * HEAD_DIM, bytes_accessed=8 * part * HEAD_DIM, transcendentals=2 * rows * part
        ),
    )(q, *pieces * 2, bias, *(() if first else before))


def combine_body(mine, mine_stat, theirs, theirs_stat, live, out):
    def joined(at):
        parts = theirs_stat[at : at + 8, :].astype(F32)
        return parts[0:1] + parts[1:2] + parts[2:3]

    top_mine, top_theirs = mine_stat[0:1], joined(0)
    top = jnp.maximum(top_mine, top_theirs)
    part_mine = mine_stat[4:5] * jnp.exp2(top_mine - top)
    part_theirs = joined(8) * jnp.exp2(top_theirs - top)
    factor = live[...] / (part_mine + part_theirs)
    tile = out.shape[0]

    def down(row):
        wide = jnp.broadcast_to(row, (128, tile)).T
        return jnp.concatenate([wide, wide], axis=1)

    out[...] = (mine[...] * down(part_mine * factor) + theirs[...].astype(F32) * down(part_theirs * factor)).astype(BF)


def combine(mine, mine_stat, theirs, live):
    rows = mine.shape[0]
    tile = 256
    return pl.pallas_call(
        combine_body,
        grid=(rows // tile,),
        in_specs=[
            pl.BlockSpec((tile, HEAD_DIM), lambda i: (i, 0)),
            pl.BlockSpec((8, tile), lambda i: (0, i)),
            pl.BlockSpec((tile, HEAD_DIM), lambda i: (i, 0)),
            pl.BlockSpec((16, tile), lambda i: (rows // 16 + i, 0)),
            pl.BlockSpec((1, tile), lambda i: (0, i)),
        ],
        out_specs=pl.BlockSpec((tile, HEAD_DIM), lambda i: (i, 0)),
        out_shape=jax.ShapeDtypeStruct((rows, HEAD_DIM), BF),
        compiler_params=pltpu.CompilerParams(vmem_limit_bytes=VMEM // 2),
    )(mine, mine_stat, theirs, theirs, live)


def columns_body(grad, swap, out):
    for xh in range(2):
        for zq in range(4):
            at = (xh * 4 + zq) * 256
            both = jnp.dot(grad[:, at : at + 256], swap[...], preferred_element_type=F32).astype(BF)
            for xl in range(2):
                out[xh, xl, :, zq * 128 : (zq + 1) * 128] = both[:, xl * 128 : (xl + 1) * 128]


def by_owner(grad):
    rows, width = grad.shape
    place = jnp.arange(256)
    source = place % 128 // 32 * 64 + place // 128 * 32 + place % 32
    swap = (place[:, None] == source[None, :]).astype(BF)
    return pl.pallas_call(
        columns_body,
        out_shape=jax.ShapeDtypeStruct((2, 2, rows, width // 4), BF),
        compiler_params=pltpu.CompilerParams(vmem_limit_bytes=VMEM // 2),
        cost_estimate=pl.CostEstimate(flops=2 * rows * width * 256, bytes_accessed=2**19, transcendentals=0),
    )(grad, swap)


def beside(value, dh, dl):
    return moved(value, xh=dh, xl=dl) if dh or dl else value


def local(query_rows, key_rows, value_rows, seq_length, out_weight, out_grad):
    query, key, value = query_rows[0], key_rows[0], value_rows[0]
    length = seq_length[0]
    count = query.shape[0]
    xh, zq, zr, core, y, xl = (lax.axis_index(n) for n in AXES)

    def head_of(array, steps):
        return lax.dynamic_slice_in_dim(array, ((zq + steps) % 4) * HEAD_DIM, HEAD_DIM, 1)

    sent = {d: jnp.concatenate([head_of(key, d), head_of(query, d), head_of(value, d)]) for d in range(4)}
    sent = {d: moved(sent[d], zq=d) if d else sent[d] for d in (1, 3, 2, 0)}
    k_own, q_own, v_own = (
        jnp.concatenate([sent[d][i * count : (i + 1) * count] for d in range(4)]) for i in range(3)
    )
    rows, width = out_grad.shape[1:]
    grad = by_owner(out_grad[0])

    sides = ((0, 0), (0, 1), (1, 1), (1, 0))

    def for_x(dh, dl):
        part = lax.dynamic_index_in_dim(grad, (xh + dh) % 2, 0, keepdims=False)
        return lax.dynamic_index_in_dim(part, (xl + dl) % 2, 0, keepdims=False)

    grad = jnp.stack([beside(for_x(*side), *side) for side in sides])

    def positions(xh, zr, core):
        source = (zq - jnp.arange(4)) % 4
        block = xh * 16 + source * 4 + zr * 2 + core
        return (block[:, None] * count + jnp.arange(count)[None, :]).reshape(-1)

    key_place = jnp.concatenate(
        [positions(xh, zr, core), positions(xh, zr, 1 - core), positions(1 - xh, zr, core), positions(1 - xh, zr, 1 - core)]
    )
    bias = jnp.where(key_place < length, 0.0, MASKED).astype(F32)[None, :]
    live = (positions(xh, zr, core) < length).astype(F32)[None, :]
    grad_y = {0: grad, 1: moved(grad, y=1), 3: moved(grad, y=3)}
    k_own, q_own, v_own, bias, live, grad_y = lax.optimization_barrier((k_own, q_own, v_own, bias, live, grad_y))

    own = jnp.concatenate([k_own, v_own])
    other = moved(own, xh=1)
    q_other = moved(q_own, zr=1)
    here = (own, moved(own, core=1))
    begun = attend(q_other, here, bias), attend(q_own, here, bias)
    other, begun = lax.optimization_barrier((other, begun))
    there = (other, moved(other, core=1))
    theirs = attend(q_other, there, bias, begun[0], packed=True)
    theirs = moved(theirs, zr=1)
    mine, mine_stat = attend(q_own, there, bias, begun[1])
    grad_y[2] = moved(after(grad_y[0], mine_stat), y=2)
    context = combine(mine, mine_stat, theirs, live)

    back = context.reshape(4, count, HEAD_DIM)
    mine_back = jnp.zeros((count, 4 * HEAD_DIM), BF)
    for d in (0, 1, 3, 2):
        part = moved(back[d], zq=-d) if d else back[d]
        mine_back = lax.dynamic_update_slice_in_dim(mine_back, part, ((zq + d) % 4) * HEAD_DIM, 1)

    grad_y[2] = after(grad_y[2], context)
    grad_rows = jnp.zeros((4, 4, rows, width // 4), BF)
    for d in range(4):
        grad_rows = lax.dynamic_update_index_in_dim(grad_rows, grad_y[d], (y - d) % 4, 1)
    grad_rows = grad_rows.reshape(16 * rows, width // 4)

    gathered = jnp.concatenate([beside(mine_back, *side) for side in sides])
    projected = jnp.dot(mine_back, out_weight, preferred_element_type=F32).astype(BF).reshape(4, rows, width)
    gathered, projected = lax.optimization_barrier((gathered, projected))
    total = lax.dot_general(grad_rows, gathered, (((0,), (0,)), ((), ())), preferred_element_type=F32)
    total = total.reshape(4, 2, 2, 32, 4 * HEAD_DIM)
    for axis, name, place in ((2, "core", core), (1, "zr", zr)):
        keep = lax.dynamic_index_in_dim(total, place, axis, keepdims=False)
        give = lax.dynamic_index_in_dim(total, 1 - place, axis, keepdims=False)
        total = keep + moved(give.astype(BF), **{name: 1}).astype(F32)
    weight_grad = lax.dynamic_index_in_dim(total, zq, 0, keepdims=False)
    for d in (1, 3, 2):
        part = lax.dynamic_index_in_dim(total, (zq + d) % 4, 0, keepdims=False)
        weight_grad += moved(part.astype(BF), zq=d).astype(F32)


    def for_y(steps):
        return lax.dynamic_index_in_dim(projected, (y + steps) % 4, 0, keepdims=False)

    block = for_y(0).astype(F32)
    for d in (1, 3, 2):
        block += moved(for_y(d), y=d).astype(F32)
    return block.astype(BF)[None], weight_grad.T


def solution(mesh):
    fine = Mesh(mesh.devices.reshape([s for _, s in SPLIT]), AXES)
    ctx = ("xh", "zq", "zr", "core")
    in_specs = (
        P("xl", ctx, "y"),
        P("xl", ctx, "y"),
        P("xl", ctx, "y"),
        P("xl"),
        P("y", None),
        P("xl", ctx + ("y",), None),
    )
    out_specs = (P("xl", ctx + ("y",), None), P("y", ctx + ("xl",)))
    return jax.shard_map(local, mesh=fine, in_specs=in_specs, out_specs=out_specs, check_vma=False)
```

```python
import functools
import math

import jax
import jax.numpy as jnp
from jax import lax
from jax.experimental import pallas as pl
from jax.experimental.pallas import tpu as pltpu
from jax.sharding import Mesh, PartitionSpec as P

HEAD_DIM = 256
SPLIT = (("xh", 2), ("zq", 4), ("zr", 2), ("core", 2), ("y", 4), ("xl", 2))
AXES = tuple(name for name, _ in SPLIT)
SIZE = dict(SPLIT)
MASKED = -1e30
BF = jnp.bfloat16
F32 = jnp.float32
VMEM = 14 * 2**20


def moved(value, **shift):
    names = tuple(shift)
    sizes = [SIZE[n] for n in names]
    count = math.prod(sizes)
    pairs = []
    for source in range(count):
        rest, place = source, []
        for s in reversed(sizes):
            place.append(rest % s)
            rest //= s
        place = place[::-1]
        target = 0
        for p, s, n in zip(place, sizes, names):
            target = target * s + (p + shift[n]) % s
        pairs.append((source, target))
    return lax.ppermute(value, names, pairs)


def after(value, *earlier):
    return lax.optimization_barrier((value, *earlier))[0]


def attend_body(q_ref, k0, k1, v0, v1, bias, *refs, first, packed):
    tile = q_ref.shape[0]
    q = q_ref[...]
    if first:
        out, stat_out = refs
        acc = jnp.zeros((tile, HEAD_DIM), F32)
        total = jnp.zeros((tile, 1), F32)
        top = jnp.full((tile, 1), -jnp.inf, F32)
    else:
        acc_in, stat_in, out, *stat_out = refs

        def down(row):
            return jnp.broadcast_to(row, (128, tile)).T[:, :1]

        top, total = down(stat_in[0:1]), down(stat_in[4:5])
    parts = []
    new_top = top
    for i, k in enumerate((k0, k1)):
        s = lax.dot_general(q, k[...], (((1,), (1,)), ((), ())), preferred_element_type=F32)
        width = k.shape[0]
        parts.append(s * (math.log2(math.e) / math.sqrt(HEAD_DIM)) + bias[:, i * width : (i + 1) * width])
        new_top = jnp.maximum(new_top, parts[-1].max(axis=1, keepdims=True))
    if not first:
        fade = jnp.exp2(top - new_top)
        total = total * fade
        acc = acc_in[...] * fade
    top = new_top
    for s, v in zip(parts, (v0, v1)):
        e = jnp.exp2(s - top)
        total += e.sum(axis=1, keepdims=True)
        acc += jnp.dot(e.astype(BF), v[...], preferred_element_type=F32)
    if not packed:
        out[...] = acc if first else acc / total
        stat_out = stat_out if first else stat_out[0]
        stat_out[:4, :] = jnp.broadcast_to(top, (tile, 128)).T[:4]
        stat_out[4:, :] = jnp.broadcast_to(total, (tile, 128)).T[:4]
        return
    step = pl.program_id(0)
    out[pl.ds(pl.multiple_of(step * tile, tile), tile), :] = (acc / total).astype(BF)
    lines = []
    for stat in (top, total):
        left = jnp.broadcast_to(stat, (tile, 128)).T[:1]
        for _ in range(3):
            lines.append(left.astype(BF).astype(F32))
            left = left - lines[-1]
        lines.append(jnp.zeros((5, tile), F32))
    below = pl.multiple_of(pl.num_programs(0) * tile + step * 16, 16)
    out[pl.ds(below, 16), :] = jnp.concatenate(lines).astype(BF)


def attend(q, pieces, bias, before=None, packed=False):
    rows = q.shape[0]
    tile = 256
    steps = rows // tile
    part = pieces[0].shape[0] // 2
    first = before is None
    rows_spec = pl.BlockSpec((tile, HEAD_DIM), lambda i: (i, 0))
    stat_spec = pl.BlockSpec((8, tile), lambda i: (0, i))
    if packed:
        out_shape = jax.ShapeDtypeStruct((rows + 16 * steps, HEAD_DIM), BF)
        out_specs = pl.BlockSpec(out_shape.shape, lambda i: (0, 0))
    else:
        out_specs = [rows_spec, stat_spec]
        out_shape = [jax.ShapeDtypeStruct((rows, HEAD_DIM), F32), jax.ShapeDtypeStruct((8, rows), F32)]
    return pl.pallas_call(
        functools.partial(attend_body, first=first, packed=packed),
        grid=(steps,),
        in_specs=[rows_spec]
        + [pl.BlockSpec((part, HEAD_DIM), lambda i, at=at: (at, 0)) for at in (0, 0, 1, 1)]
        + [pl.BlockSpec((1, 2 * part), lambda i: (0, 0 if first else 1))]
        + ([] if first else [rows_spec, stat_spec]),
        out_specs=out_specs,
        out_shape=out_shape,
        compiler_params=pltpu.CompilerParams(vmem_limit_bytes=VMEM),
        cost_estimate=pl.CostEstimate(
            flops=8 * rows * part * HEAD_DIM, bytes_accessed=8 * part * HEAD_DIM, transcendentals=2 * rows * part
        ),
    )(q, *pieces * 2, bias, *(() if first else before))


def combine_body(mine, mine_stat, theirs, theirs_stat, live, out):
    def joined(at):
        parts = theirs_stat[at : at + 8, :].astype(F32)
        return parts[0:1] + parts[1:2] + parts[2:3]

    top_mine, top_theirs = mine_stat[0:1], joined(0)
    top = jnp.maximum(top_mine, top_theirs)
    part_mine = mine_stat[4:5] * jnp.exp2(top_mine - top)
    part_theirs = joined(8) * jnp.exp2(top_theirs - top)
    factor = live[...] / (part_mine + part_theirs)
    tile = out.shape[0]

    def down(row):
        wide = jnp.broadcast_to(row, (128, tile)).T
        return jnp.concatenate([wide, wide], axis=1)

    out[...] = (mine[...] * down(part_mine * factor) + theirs[...].astype(F32) * down(part_theirs * factor)).astype(BF)


def combine(mine, mine_stat, theirs, live):
    rows = mine.shape[0]
    tile = 256
    return pl.pallas_call(
        combine_body,
        grid=(rows // tile,),
        in_specs=[
            pl.BlockSpec((tile, HEAD_DIM), lambda i: (i, 0)),
            pl.BlockSpec((8, tile), lambda i: (0, i)),
            pl.BlockSpec((tile, HEAD_DIM), lambda i: (i, 0)),
            pl.BlockSpec((16, tile), lambda i: (rows // 16 + i, 0)),
            pl.BlockSpec((1, tile), lambda i: (0, i)),
        ],
        out_specs=pl.BlockSpec((tile, HEAD_DIM), lambda i: (i, 0)),
        out_shape=jax.ShapeDtypeStruct((rows, HEAD_DIM), BF),
        compiler_params=pltpu.CompilerParams(vmem_limit_bytes=VMEM // 2),
    )(mine, mine_stat, theirs, theirs, live)


def columns_body(grad, swap, earlier, out):
    for xh in range(2):
        for zq in range(4):
            at = (xh * 4 + zq) * 256
            both = jnp.dot(grad[:, at : at + 256], swap[...], preferred_element_type=F32).astype(BF)
            for xl in range(2):
                for core in range(2):
                    at, to = xl * 128 + core * 64, core * 256 + zq * 64
                    out[xh, xl, :, to : to + 64] = both[:, at : at + 64]


def by_owner(grad, earlier):
    rows, width = grad.shape
    place = jnp.arange(256)
    source = place % 64 // 32 * 128 + place % 128 // 64 * 64 + place // 128 * 32 + place % 32
    swap = (place[:, None] == source[None, :]).astype(BF)
    whole = pl.BlockSpec(memory_space=pltpu.VMEM)
    return pl.pallas_call(
        columns_body,
        in_specs=[whole, whole, pl.BlockSpec(memory_space=pl.ANY)],
        out_specs=whole,
        out_shape=jax.ShapeDtypeStruct((2, 2, rows, width // 4), BF),
        compiler_params=pltpu.CompilerParams(vmem_limit_bytes=VMEM // 2),
        cost_estimate=pl.CostEstimate(flops=2 * rows * width * 256, bytes_accessed=2**19, transcendentals=0),
    )(grad, swap, earlier)


def beside(value, dh, dl):
    return moved(value, xh=dh, xl=dl) if dh or dl else value


def local(query_rows, key_rows, value_rows, seq_length, out_weight, out_grad):
    query, key, value = query_rows[0], key_rows[0], value_rows[0]
    length = seq_length[0]
    count = query.shape[0]
    xh, zq, zr, core, y, xl = (lax.axis_index(n) for n in AXES)

    def head_of(array, steps):
        return lax.dynamic_slice_in_dim(array, ((zq + steps) % 4) * HEAD_DIM, HEAD_DIM, 1)

    sent = {d: jnp.concatenate([head_of(key, d), head_of(query, d), head_of(value, d)]) for d in range(4)}
    owned = by_owner(out_grad[0], sent[2])
    sent[3] = after(sent[3], owned)
    sent = {d: moved(sent[d], zq=d) if d else sent[d] for d in (1, 3, 2, 0)}
    k_own, q_own, v_own = (
        jnp.concatenate([sent[d][i * count : (i + 1) * count] for d in range(4)]) for i in range(3)
    )
    rows, width = out_grad.shape[1:]
    grad = owned

    sides = ((0, 0), (0, 1), (1, 1), (1, 0))

    def for_x(dh, dl):
        part = lax.dynamic_index_in_dim(grad, (xh + dh) % 2, 0, keepdims=False)
        return lax.dynamic_index_in_dim(part, (xl + dl) % 2, 0, keepdims=False)

    grad = jnp.stack([beside(for_x(*side), *side) for side in sides])

    def positions(xh, zr, core):
        source = (zq - jnp.arange(4)) % 4
        block = xh * 16 + source * 4 + zr * 2 + core
        return (block[:, None] * count + jnp.arange(count)[None, :]).reshape(-1)

    key_place = jnp.concatenate(
        [positions(xh, zr, core), positions(xh, zr, 1 - core), positions(1 - xh, zr, core), positions(1 - xh, zr, 1 - core)]
    )
    bias = jnp.where(key_place < length, 0.0, MASKED).astype(F32)[None, :]
    live = (positions(xh, zr, core) < length).astype(F32)[None, :]
    grad_y = {0: grad, 1: moved(grad, y=1), 3: moved(grad, y=3)}
    k_own, q_own, v_own, bias, live, grad_y = lax.optimization_barrier((k_own, q_own, v_own, bias, live, grad_y))

    own = jnp.concatenate([k_own, v_own])
    other = moved(own, xh=1)
    q_other = moved(q_own, zr=1)
    here = (own, moved(own, core=1))
    begun = attend(q_other, here, bias), attend(q_own, here, bias)
    other, begun = lax.optimization_barrier((other, begun))
    there = (other, moved(other, core=1))
    theirs = attend(q_other, there, bias, begun[0], packed=True)
    theirs = moved(theirs, zr=1)
    mine, mine_stat = attend(q_own, there, bias, begun[1])
    grad_y[2] = moved(after(grad_y[0], mine_stat), y=2)
    context = combine(mine, mine_stat, theirs, live)

    back = context.reshape(4, count, HEAD_DIM)
    mine_back = jnp.zeros((count, 4 * HEAD_DIM), BF)
    for d in (0, 1, 3, 2):
        part = moved(back[d], zq=-d) if d else back[d]
        mine_back = lax.dynamic_update_slice_in_dim(mine_back, part, ((zq + d) % 4) * HEAD_DIM, 1)

    grad_y[2] = after(grad_y[2], context)
    grad_rows = jnp.zeros((4, 4, rows, width // 4), BF)
    for d in range(4):
        grad_rows = lax.dynamic_update_index_in_dim(grad_rows, grad_y[d], (y - d) % 4, 1)
    grad_rows = grad_rows.reshape(16 * rows, width // 4)

    half = grad_rows.shape[1] // 2
    give = lax.dynamic_slice_in_dim(grad_rows, (1 - core) * half, half, 1)
    keep = lax.dynamic_slice_in_dim(grad_rows, core * half, half, 1)
    grad_rows = jnp.concatenate([keep, moved(after(give, mine_back), core=1)])
    gathered = [beside(mine_back, *side) for side in sides]
    gathered = jnp.concatenate(gathered + [moved(part, core=1) for part in gathered])
    projected = jnp.dot(mine_back, out_weight, preferred_element_type=F32).astype(BF).reshape(4, rows, width)
    gathered, projected = lax.optimization_barrier((gathered, projected))
    total = lax.dot_general(grad_rows, gathered, (((0,), (0,)), ((), ())), preferred_element_type=F32)
    total = total.reshape(4, 2, 32, 4 * HEAD_DIM)
    keep = lax.dynamic_index_in_dim(total, zr, 1, keepdims=False)
    give = lax.dynamic_index_in_dim(total, 1 - zr, 1, keepdims=False)
    total = keep + moved(give.astype(BF), zr=1).astype(F32)
    weight_grad = lax.dynamic_index_in_dim(total, zq, 0, keepdims=False)
    for d in (1, 3, 2):
        part = lax.dynamic_index_in_dim(total, (zq + d) % 4, 0, keepdims=False)
        weight_grad += moved(part.astype(BF), zq=d).astype(F32)


    def for_y(steps):
        return lax.dynamic_index_in_dim(projected, (y + steps) % 4, 0, keepdims=False)

    block = for_y(0).astype(F32)
    for d in (1, 3, 2):
        block += moved(for_y(d), y=d).astype(F32)
    return block.astype(BF)[None], weight_grad.T


def solution(mesh):
    fine = Mesh(mesh.devices.reshape([s for _, s in SPLIT]), AXES)
    ctx = ("xh", "zq", "zr", "core")
    in_specs = (
        P("xl", ctx, "y"),
        P("xl", ctx, "y"),
        P("xl", ctx, "y"),
        P("xl"),
        P("y", None),
        P("xl", ctx + ("y",), None),
    )
    out_specs = (P("xl", ctx + ("y",), None), P("y", ctx + ("xl",)))
    return jax.shard_map(local, mesh=fine, in_specs=in_specs, out_specs=out_specs, check_vma=False)
```

```python
import functools
import math

import jax
import jax.numpy as jnp
from jax import lax
from jax.experimental import pallas as pl
from jax.experimental.pallas import tpu as pltpu
from jax.sharding import Mesh, PartitionSpec as P

HEAD_DIM = 256
SPLIT = (("xh", 2), ("zq", 4), ("zr", 2), ("core", 2), ("y", 4), ("xl", 2))
AXES = tuple(name for name, _ in SPLIT)
SIZE = dict(SPLIT)
MASKED = -1e30
BF = jnp.bfloat16
F32 = jnp.float32
VMEM = 14 * 2**20


def moved(value, **shift):
    names = tuple(shift)
    sizes = [SIZE[n] for n in names]
    count = math.prod(sizes)
    pairs = []
    for source in range(count):
        rest, place = source, []
        for s in reversed(sizes):
            place.append(rest % s)
            rest //= s
        place = place[::-1]
        target = 0
        for p, s, n in zip(place, sizes, names):
            target = target * s + (p + shift[n]) % s
        pairs.append((source, target))
    return lax.ppermute(value, names, pairs)


def after(value, *earlier):
    return lax.optimization_barrier((value, *earlier))[0]


def attend_body(q_ref, *refs, first, packed, blocks):
    tile = q_ref.shape[0]
    q = q_ref[...]
    keys, values, bias, refs = refs[:blocks], refs[blocks : 2 * blocks], refs[2 * blocks], refs[2 * blocks + 1 :]
    if first:
        out, stat_out = refs
        acc = jnp.zeros((tile, HEAD_DIM), F32)
        total = jnp.zeros((tile, 1), F32)
        top = jnp.full((tile, 1), -jnp.inf, F32)
    else:
        acc_in, stat_in, out, *stat_out = refs

        def down(row):
            return jnp.broadcast_to(row, (128, tile)).T[:, :1]

        top, total = down(stat_in[0:1]), down(stat_in[4:5])
    parts = []
    new_top = top
    for i, k in enumerate(keys):
        s = lax.dot_general(q, k[...], (((1,), (1,)), ((), ())), preferred_element_type=F32)
        width = k.shape[0]
        parts.append(s * (math.log2(math.e) / math.sqrt(HEAD_DIM)) + bias[:, i * width : (i + 1) * width])
        new_top = jnp.maximum(new_top, parts[-1].max(axis=1, keepdims=True))
    if not first:
        fade = jnp.exp2(top - new_top)
        total = total * fade
        acc = acc_in[...] * fade
    top = new_top
    for s, v in zip(parts, values):
        e = jnp.exp2(s - top)
        total += e.sum(axis=1, keepdims=True)
        acc += jnp.dot(e.astype(BF), v[...], preferred_element_type=F32)
    if not packed:
        out[...] = acc
        stat_out = stat_out if first else stat_out[0]
        stat_out[:4, :] = jnp.broadcast_to(top, (tile, 128)).T[:4]
        stat_out[4:, :] = jnp.broadcast_to(total, (tile, 128)).T[:4]
        return
    step = pl.program_id(0)
    out[pl.ds(pl.multiple_of(step * tile, tile), tile), :] = (acc / total).astype(BF)
    lines = []
    for stat in (top, total):
        left = jnp.broadcast_to(stat, (tile, 128)).T[:1]
        for _ in range(3):
            lines.append(left.astype(BF).astype(F32))
            left = left - lines[-1]
        lines.append(jnp.zeros((5, tile), F32))
    below = pl.multiple_of(pl.num_programs(0) * tile + step * 16, 16)
    out[pl.ds(below, 16), :] = jnp.concatenate(lines).astype(BF)


def attend(q, pieces, bias, at=0, before=None, packed=False):
    rows = q.shape[0]
    tile = 256
    steps = rows // tile
    part = pieces[0].shape[0] // 2
    first = before is None
    rows_spec = pl.BlockSpec((tile, HEAD_DIM), lambda i: (i, 0))
    stat_spec = pl.BlockSpec((8, tile), lambda i: (0, i))
    if packed:
        out_shape = jax.ShapeDtypeStruct((rows + 16 * steps, HEAD_DIM), BF)
        out_specs = pl.BlockSpec(out_shape.shape, lambda i: (0, 0))
    else:
        out_specs = [rows_spec, stat_spec]
        out_shape = [jax.ShapeDtypeStruct((rows, HEAD_DIM), F32), jax.ShapeDtypeStruct((8, rows), F32)]
    return pl.pallas_call(
        functools.partial(attend_body, first=first, packed=packed, blocks=len(pieces)),
        grid=(steps,),
        in_specs=[rows_spec]
        + [pl.BlockSpec((part, HEAD_DIM), lambda i, at=at: (at, 0)) for at in (0,) * len(pieces) + (1,) * len(pieces)]
        + [pl.BlockSpec((1, len(pieces) * part), lambda i: (0, at))]
        + ([] if first else [rows_spec, stat_spec]),
        out_specs=out_specs,
        out_shape=out_shape,
        compiler_params=pltpu.CompilerParams(vmem_limit_bytes=VMEM),
        cost_estimate=pl.CostEstimate(
            flops=4 * len(pieces) * rows * part * HEAD_DIM,
            bytes_accessed=4 * len(pieces) * part * HEAD_DIM,
            transcendentals=len(pieces) * rows * part,
        ),
    )(q, *pieces * 2, bias, *(() if first else before))


def combine_body(mine, mine_stat, theirs, theirs_stat, live, out):
    def joined(at):
        parts = theirs_stat[at : at + 8, :].astype(F32)
        return parts[0:1] + parts[1:2] + parts[2:3]

    top_mine, top_theirs = mine_stat[0:1], joined(0)
    top = jnp.maximum(top_mine, top_theirs)
    fade_mine = jnp.exp2(top_mine - top)
    part_mine = mine_stat[4:5] * fade_mine
    part_theirs = joined(8) * jnp.exp2(top_theirs - top)
    factor = live[...] / (part_mine + part_theirs)
    tile = out.shape[0]

    def down(row):
        wide = jnp.broadcast_to(row, (128, tile)).T
        return jnp.concatenate([wide, wide], axis=1)

    out[...] = (mine[...] * down(fade_mine * factor) + theirs[...].astype(F32) * down(part_theirs * factor)).astype(BF)


def combine(mine, mine_stat, theirs, live):
    rows = mine.shape[0]
    tile = 256
    return pl.pallas_call(
        combine_body,
        grid=(rows // tile,),
        in_specs=[
            pl.BlockSpec((tile, HEAD_DIM), lambda i: (i, 0)),
            pl.BlockSpec((8, tile), lambda i: (0, i)),
            pl.BlockSpec((tile, HEAD_DIM), lambda i: (i, 0)),
            pl.BlockSpec((16, tile), lambda i: (rows // 16 + i, 0)),
            pl.BlockSpec((1, tile), lambda i: (0, i)),
        ],
        out_specs=pl.BlockSpec((tile, HEAD_DIM), lambda i: (i, 0)),
        out_shape=jax.ShapeDtypeStruct((rows, HEAD_DIM), BF),
        compiler_params=pltpu.CompilerParams(vmem_limit_bytes=VMEM // 2),
    )(mine, mine_stat, theirs, theirs, live)


def columns_body(grad, swap, earlier, out):
    for xh in range(2):
        for zq in range(4):
            at = (xh * 4 + zq) * 256
            both = jnp.dot(grad[:, at : at + 256], swap[...], preferred_element_type=F32).astype(BF)
            for xl in range(2):
                for core in range(2):
                    at, to = xl * 128 + core * 64, core * 256 + zq * 64
                    out[xh, xl, :, to : to + 64] = both[:, at : at + 64]


def by_owner(grad, earlier):
    rows, width = grad.shape
    place = jnp.arange(256)
    source = place % 64 // 32 * 128 + place % 128 // 64 * 64 + place // 128 * 32 + place % 32
    swap = (place[:, None] == source[None, :]).astype(BF)
    whole = pl.BlockSpec(memory_space=pltpu.VMEM)
    return pl.pallas_call(
        columns_body,
        in_specs=[whole, whole, pl.BlockSpec(memory_space=pl.ANY)],
        out_specs=whole,
        out_shape=jax.ShapeDtypeStruct((2, 2, rows, width // 4), BF),
        compiler_params=pltpu.CompilerParams(vmem_limit_bytes=VMEM // 2),
        cost_estimate=pl.CostEstimate(flops=2 * rows * width * 256, bytes_accessed=2**19, transcendentals=0),
    )(grad, swap, earlier)


def beside(value, dh, dl):
    return moved(value, xh=dh, xl=dl) if dh or dl else value


def local(query_rows, key_rows, value_rows, seq_length, out_weight, out_grad):
    query, key, value = query_rows[0], key_rows[0], value_rows[0]
    length = seq_length[0]
    count = query.shape[0]
    xh, zq, zr, core, y, xl = (lax.axis_index(n) for n in AXES)

    def head_of(array, steps):
        return lax.dynamic_slice_in_dim(array, ((zq + steps) % 4) * HEAD_DIM, HEAD_DIM, 1)

    sent = {d: jnp.concatenate([head_of(key, d), head_of(query, d), head_of(value, d)]) for d in range(4)}
    owned = by_owner(out_grad[0], sent[2])
    sent[3] = after(sent[3], owned)
    sent = {d: moved(sent[d], zq=d) if d else sent[d] for d in (1, 3, 2, 0)}
    k_own, q_own, v_own = (
        jnp.concatenate([sent[d][i * count : (i + 1) * count] for d in range(4)]) for i in range(3)
    )
    rows, width = out_grad.shape[1:]
    grad = owned

    sides = ((0, 0), (0, 1), (1, 1), (1, 0))

    def for_x(dh, dl):
        part = lax.dynamic_index_in_dim(grad, (xh + dh) % 2, 0, keepdims=False)
        return lax.dynamic_index_in_dim(part, (xl + dl) % 2, 0, keepdims=False)

    grad = jnp.stack([beside(for_x(*side), *side) for side in sides])

    def positions(xh, zr, core):
        source = (zq - jnp.arange(4)) % 4
        block = xh * 16 + source * 4 + zr * 2 + core
        return (block[:, None] * count + jnp.arange(count)[None, :]).reshape(-1)

    key_place = jnp.concatenate(
        [positions(xh, zr, core), positions(xh, zr, 1 - core), positions(1 - xh, zr, core), positions(1 - xh, zr, 1 - core)]
    )
    bias = jnp.where(key_place < length, 0.0, MASKED).astype(F32)[None, :]
    live = (positions(xh, zr, core) < length).astype(F32)[None, :]
    grad_y = {0: grad, 1: moved(grad, y=1), 3: moved(grad, y=3)}
    k_own, q_own, v_own, bias, live, grad_y = lax.optimization_barrier((k_own, q_own, v_own, bias, live, grad_y))

    own = jnp.concatenate([k_own, v_own])
    other = moved(own, xh=1)
    q_other = moved(q_own, zr=1)
    here = (own, moved(own, core=1))
    begun = attend(q_other, here, bias), attend(q_own, here, bias)
    other, begun = lax.optimization_barrier((other, begun))
    there = moved(other, core=1)
    theirs = attend(q_other, (there,), bias, 3, attend(q_other, (other,), bias, 2, begun[0]), packed=True)
    theirs = moved(theirs, zr=1)
    mine, mine_stat = attend(q_own, (other, there), bias, 1, begun[1])
    grad_y[2] = moved(after(grad_y[0], mine_stat), y=2)
    context = combine(mine, mine_stat, theirs, live)

    back = context.reshape(4, count, HEAD_DIM)
    mine_back = jnp.zeros((count, 4 * HEAD_DIM), BF)
    for d in (0, 1, 3, 2):
        part = moved(back[d], zq=-d) if d else back[d]
        mine_back = lax.dynamic_update_slice_in_dim(mine_back, part, ((zq + d) % 4) * HEAD_DIM, 1)

    grad_y[2] = after(grad_y[2], context)
    grad_rows = jnp.zeros((4, 4, rows, width // 4), BF)
    for d in range(4):
        grad_rows = lax.dynamic_update_index_in_dim(grad_rows, grad_y[d], (y - d) % 4, 1)
    grad_rows = grad_rows.reshape(16 * rows, width // 4)

    half = grad_rows.shape[1] // 2
    give = lax.dynamic_slice_in_dim(grad_rows, (1 - core) * half, half, 1)
    keep = lax.dynamic_slice_in_dim(grad_rows, core * half, half, 1)
    grad_rows = jnp.concatenate([keep, moved(after(give, mine_back), core=1)])
    gathered = [beside(mine_back, *side) for side in sides]
    gathered = jnp.concatenate(gathered + [moved(part, core=1) for part in gathered])
    projected = jnp.dot(mine_back, out_weight, preferred_element_type=F32).astype(BF).reshape(4, rows, width)
    gathered, projected = lax.optimization_barrier((gathered, projected))
    total = lax.dot_general(grad_rows, gathered, (((0,), (0,)), ((), ())), preferred_element_type=F32)
    total = total.reshape(4, 2, 32, 4 * HEAD_DIM)
    keep = lax.dynamic_index_in_dim(total, zr, 1, keepdims=False)
    give = lax.dynamic_index_in_dim(total, 1 - zr, 1, keepdims=False)
    total = keep + moved(give.astype(BF), zr=1).astype(F32)
    weight_grad = lax.dynamic_index_in_dim(total, zq, 0, keepdims=False)
    for d in (1, 3, 2):
        part = lax.dynamic_index_in_dim(total, (zq + d) % 4, 0, keepdims=False)
        weight_grad += moved(part.astype(BF), zq=d).astype(F32)


    def for_y(steps):
        return lax.dynamic_index_in_dim(projected, (y + steps) % 4, 0, keepdims=False)

    block = for_y(0).astype(F32)
    for d in (1, 3, 2):
        block += moved(for_y(d), y=d).astype(F32)
    return block.astype(BF)[None], weight_grad.T


def solution(mesh):
    fine = Mesh(mesh.devices.reshape([s for _, s in SPLIT]), AXES)
    ctx = ("xh", "zq", "zr", "core")
    in_specs = (
        P("xl", ctx, "y"),
        P("xl", ctx, "y"),
        P("xl", ctx, "y"),
        P("xl"),
        P("y", None),
        P("xl", ctx + ("y",), None),
    )
    out_specs = (P("xl", ctx + ("y",), None), P("y", ctx + ("xl",)))
    return jax.shard_map(local, mesh=fine, in_specs=in_specs, out_specs=out_specs, check_vma=False)
```

```python
import functools
import math

import jax
import jax.numpy as jnp
from jax import lax
from jax.experimental import pallas as pl
from jax.experimental.pallas import tpu as pltpu
from jax.sharding import Mesh, PartitionSpec as P

HEAD_DIM = 256
SPLIT = (("xh", 2), ("zq", 4), ("zr", 2), ("core", 2), ("y", 4), ("xl", 2))
AXES = tuple(name for name, _ in SPLIT)
SIZE = dict(SPLIT)
MASKED = -1e30
BF = jnp.bfloat16
F32 = jnp.float32
VMEM = 14 * 2**20


def moved(value, **shift):
    names = tuple(shift)
    sizes = [SIZE[n] for n in names]
    count = math.prod(sizes)
    pairs = []
    for source in range(count):
        rest, place = source, []
        for s in reversed(sizes):
            place.append(rest % s)
            rest //= s
        place = place[::-1]
        target = 0
        for p, s, n in zip(place, sizes, names):
            target = target * s + (p + shift[n]) % s
        pairs.append((source, target))
    return lax.ppermute(value, names, pairs)


def after(value, *earlier):
    return lax.optimization_barrier((value, *earlier))[0]


def attend_body(q_ref, k0, k1, v0, v1, bias, *refs, first, packed):
    tile = q_ref.shape[0]
    q = q_ref[...]
    if first:
        out, stat_out = refs
        acc = jnp.zeros((tile, HEAD_DIM), F32)
        total = jnp.zeros((tile, 1), F32)
        top = jnp.full((tile, 1), -jnp.inf, F32)
    else:
        acc_in, stat_in, out, *stat_out = refs

        def down(row):
            return jnp.broadcast_to(row, (128, tile)).T[:, :1]

        top, total = down(stat_in[0:1]), down(stat_in[4:5])
    parts = []
    new_top = top
    for i, k in enumerate((k0, k1)):
        s = lax.dot_general(q, k[...], (((1,), (1,)), ((), ())), preferred_element_type=F32)
        width = k.shape[0]
        parts.append(s * (math.log2(math.e) / math.sqrt(HEAD_DIM)) + bias[:, i * width : (i + 1) * width])
        new_top = jnp.maximum(new_top, parts[-1].max(axis=1, keepdims=True))
    if not first:
        fade = jnp.exp2(top - new_top)
        total = total * fade
        acc = acc_in[...] * fade
    top = new_top
    for s, v in zip(parts, (v0, v1)):
        e = jnp.exp2(s - top)
        total += e.sum(axis=1, keepdims=True)
        acc += jnp.dot(e.astype(BF), v[...], preferred_element_type=F32)
    if not packed:
        out[...] = acc if first else acc / total
        stat_out = stat_out if first else stat_out[0]
        stat_out[:4, :] = jnp.broadcast_to(top, (tile, 128)).T[:4]
        stat_out[4:, :] = jnp.broadcast_to(total, (tile, 128)).T[:4]
        return
    step = pl.program_id(0)
    out[pl.ds(pl.multiple_of(step * tile, tile), tile), :] = (acc / total).astype(BF)
    lines = []
    for stat in (top, total):
        left = jnp.broadcast_to(stat, (tile, 128)).T[:1]
        for _ in range(3):
            lines.append(left.astype(BF).astype(F32))
            left = left - lines[-1]
        lines.append(jnp.zeros((5, tile), F32))
    below = pl.multiple_of(pl.num_programs(0) * tile + step * 16, 16)
    out[pl.ds(below, 16), :] = jnp.concatenate(lines).astype(BF)


def attend(q, pieces, bias, before=None, packed=False):
    rows = q.shape[0]
    tile = 256
    steps = rows // tile
    part = pieces[0].shape[0] // 2
    first = before is None
    rows_spec = pl.BlockSpec((tile, HEAD_DIM), lambda i: (i, 0))
    stat_spec = pl.BlockSpec((8, tile), lambda i: (0, i))
    if packed:
        out_shape = jax.ShapeDtypeStruct((rows + 16 * steps, HEAD_DIM), BF)
        out_specs = pl.BlockSpec(out_shape.shape, lambda i: (0, 0))
    else:
        out_specs = [rows_spec, stat_spec]
        out_shape = [jax.ShapeDtypeStruct((rows, HEAD_DIM), F32), jax.ShapeDtypeStruct((8, rows), F32)]
    return pl.pallas_call(
        functools.partial(attend_body, first=first, packed=packed),
        grid=(steps,),
        in_specs=[rows_spec]
        + [pl.BlockSpec((part, HEAD_DIM), lambda i, at=at: (at, 0)) for at in (0, 0, 1, 1)]
        + [pl.BlockSpec((1, 2 * part), lambda i: (0, 0 if first else 1))]
        + ([] if first else [rows_spec, stat_spec]),
        out_specs=out_specs,
        out_shape=out_shape,
        compiler_params=pltpu.CompilerParams(vmem_limit_bytes=VMEM),
        cost_estimate=pl.CostEstimate(
            flops=8 * rows * part * HEAD_DIM, bytes_accessed=8 * part * HEAD_DIM, transcendentals=2 * rows * part
        ),
    )(q, *pieces * 2, bias, *(() if first else before))


def combine_body(mine, mine_stat, theirs, theirs_stat, live, out):
    def joined(at):
        parts = theirs_stat[at : at + 8, :].astype(F32)
        return parts[0:1] + parts[1:2] + parts[2:3]

    top_mine, top_theirs = mine_stat[0:1], joined(0)
    top = jnp.maximum(top_mine, top_theirs)
    part_mine = mine_stat[4:5] * jnp.exp2(top_mine - top)
    part_theirs = joined(8) * jnp.exp2(top_theirs - top)
    factor = live[...] / (part_mine + part_theirs)
    tile = out.shape[0]

    def down(row):
        wide = jnp.broadcast_to(row, (128, tile)).T
        return jnp.concatenate([wide, wide], axis=1)

    out[...] = (mine[...] * down(part_mine * factor) + theirs[...].astype(F32) * down(part_theirs * factor)).astype(BF)


def combine(mine, mine_stat, theirs, live):
    rows = mine.shape[0]
    tile = 256
    return pl.pallas_call(
        combine_body,
        grid=(rows // tile,),
        in_specs=[
            pl.BlockSpec((tile, HEAD_DIM), lambda i: (i, 0)),
            pl.BlockSpec((8, tile), lambda i: (0, i)),
            pl.BlockSpec((tile, HEAD_DIM), lambda i: (i, 0)),
            pl.BlockSpec((16, tile), lambda i: (rows // 16 + i, 0)),
            pl.BlockSpec((1, tile), lambda i: (0, i)),
        ],
        out_specs=pl.BlockSpec((tile, HEAD_DIM), lambda i: (i, 0)),
        out_shape=jax.ShapeDtypeStruct((rows, HEAD_DIM), BF),
        compiler_params=pltpu.CompilerParams(vmem_limit_bytes=VMEM // 2),
    )(mine, mine_stat, theirs, theirs, live)


def columns_body(grad, swap, earlier, out):
    for xh in range(2):
        for zq in range(4):
            at = (xh * 4 + zq) * 256
            both = jnp.dot(grad[:, at : at + 256], swap[...], preferred_element_type=F32).astype(BF)
            for xl in range(2):
                for core in range(2):
                    at, to = xl * 128 + core * 64, core * 256 + zq * 64
                    out[xh, xl, :, to : to + 64] = both[:, at : at + 64]


def by_owner(grad, earlier):
    rows, width = grad.shape
    place = jnp.arange(256)
    source = place % 64 // 32 * 128 + place % 128 // 64 * 64 + place // 128 * 32 + place % 32
    swap = (place[:, None] == source[None, :]).astype(BF)
    whole = pl.BlockSpec(memory_space=pltpu.VMEM)
    return pl.pallas_call(
        columns_body,
        in_specs=[whole, whole, pl.BlockSpec(memory_space=pl.ANY)],
        out_specs=whole,
        out_shape=jax.ShapeDtypeStruct((2, 2, rows, width // 4), BF),
        compiler_params=pltpu.CompilerParams(vmem_limit_bytes=VMEM // 2),
        cost_estimate=pl.CostEstimate(flops=2 * rows * width * 256, bytes_accessed=2**19, transcendentals=0),
    )(grad, swap, earlier)


def beside(value, dh, dl):
    return moved(value, xh=dh, xl=dl) if dh or dl else value


def local(query_rows, key_rows, value_rows, seq_length, out_weight, out_grad):
    query, key, value = query_rows[0], key_rows[0], value_rows[0]
    length = seq_length[0]
    count = query.shape[0]
    xh, zq, zr, core, y, xl = (lax.axis_index(n) for n in AXES)

    def head_of(array, steps):
        return lax.dynamic_slice_in_dim(array, ((zq + steps) % 4) * HEAD_DIM, HEAD_DIM, 1)

    sent = {d: jnp.concatenate([head_of(key, d), head_of(query, d), head_of(value, d)]) for d in range(4)}
    owned = by_owner(out_grad[0], sent[2])
    sent[3] = after(sent[3], owned)
    sent = {d: moved(sent[d], zq=d) if d else sent[d] for d in (1, 3, 2, 0)}
    k_own, q_own, v_own = (
        jnp.concatenate([sent[d][i * count : (i + 1) * count] for d in range(4)]) for i in range(3)
    )
    rows, width = out_grad.shape[1:]
    grad = owned

    sides = ((0, 0), (0, 1), (1, 1), (1, 0))

    def for_x(dh, dl):
        part = lax.dynamic_index_in_dim(grad, (xh + dh) % 2, 0, keepdims=False)
        return lax.dynamic_index_in_dim(part, (xl + dl) % 2, 0, keepdims=False)

    grad = jnp.stack([beside(for_x(*side), *side) for side in sides])

    def positions(xh, zr, core):
        source = (zq - jnp.arange(4)) % 4
        block = xh * 16 + source * 4 + zr * 2 + core
        return (block[:, None] * count + jnp.arange(count)[None, :]).reshape(-1)

    key_place = jnp.concatenate(
        [positions(xh, zr, core), positions(xh, zr, 1 - core), positions(1 - xh, zr, core), positions(1 - xh, zr, 1 - core)]
    )
    bias = jnp.where(key_place < length, 0.0, MASKED).astype(F32)[None, :]
    live = (positions(xh, zr, core) < length).astype(F32)[None, :]
    grad_y = {0: grad, 1: moved(grad, y=1), 3: moved(grad, y=3)}
    k_own, q_own, v_own, bias, live, grad_y = lax.optimization_barrier((k_own, q_own, v_own, bias, live, grad_y))

    own = jnp.concatenate([k_own, v_own])
    other = moved(own, xh=1)
    q_other = moved(q_own, zr=1)
    here = (own, moved(own, core=1))
    begun = attend(q_other, here, bias), attend(q_own, here, bias)
    other, begun = lax.optimization_barrier((other, begun))
    there = (other, moved(other, core=1))
    theirs = attend(q_other, there, bias, begun[0], packed=True)
    theirs = moved(theirs, zr=1)
    mine, mine_stat = attend(q_own, there, bias, begun[1])
    grad_y[2] = moved(after(grad_y[0], mine_stat), y=2)
    context = combine(mine, mine_stat, theirs, live)

    back = context.reshape(4, count, HEAD_DIM)
    mine_back = jnp.zeros((count, 4 * HEAD_DIM), BF)
    for d in (0, 2, 1, 3):
        part = moved(back[d], zq=-d) if d else back[d]
        mine_back = lax.dynamic_update_slice_in_dim(mine_back, part, ((zq + d) % 4) * HEAD_DIM, 1)

    grad_y[2] = after(grad_y[2], context)
    grad_rows = jnp.zeros((4, 4, rows, width // 4), BF)
    for d in range(4):
        grad_rows = lax.dynamic_update_index_in_dim(grad_rows, grad_y[d], (y - d) % 4, 1)
    grad_rows = grad_rows.reshape(16 * rows, width // 4)

    half = grad_rows.shape[1] // 2
    give = lax.dynamic_slice_in_dim(grad_rows, (1 - core) * half, half, 1)
    keep = lax.dynamic_slice_in_dim(grad_rows, core * half, half, 1)
    grad_rows = jnp.concatenate([keep, moved(after(give, mine_back), core=1)])
    gathered = [beside(mine_back, *side) for side in sides]
    gathered = jnp.concatenate(gathered + [moved(part, core=1) for part in gathered])
    projected = jnp.dot(mine_back, out_weight, preferred_element_type=F32).astype(BF).reshape(4, rows, width)
    gathered, projected = lax.optimization_barrier((gathered, projected))
    total = lax.dot_general(grad_rows, gathered, (((0,), (0,)), ((), ())), preferred_element_type=F32)
    total = total.reshape(4, 2, 32, 4 * HEAD_DIM)
    keep = lax.dynamic_index_in_dim(total, zr, 1, keepdims=False)
    give = lax.dynamic_index_in_dim(total, 1 - zr, 1, keepdims=False)
    total = keep + moved(give.astype(BF), zr=1).astype(F32)
    weight_grad = lax.dynamic_index_in_dim(total, zq, 0, keepdims=False)
    for d in (1, 3, 2):
        part = lax.dynamic_index_in_dim(total, (zq + d) % 4, 0, keepdims=False)
        weight_grad += moved(part.astype(BF), zq=d).astype(F32)


    def for_y(steps):
        return lax.dynamic_index_in_dim(projected, (y + steps) % 4, 0, keepdims=False)

    block = for_y(0).astype(F32)
    for d in (1, 3, 2):
        block += moved(for_y(d), y=d).astype(F32)
    return block.astype(BF)[None], weight_grad.T


def solution(mesh):
    fine = Mesh(mesh.devices.reshape([s for _, s in SPLIT]), AXES)
    ctx = ("xh", "zq", "zr", "core")
    in_specs = (
        P("xl", ctx, "y"),
        P("xl", ctx, "y"),
        P("xl", ctx, "y"),
        P("xl"),
        P("y", None),
        P("xl", ctx + ("y",), None),
    )
    out_specs = (P("xl", ctx + ("y",), None), P("y", ctx + ("xl",)))
    return jax.shard_map(local, mesh=fine, in_specs=in_specs, out_specs=out_specs, check_vma=False)
```
